32 devices in a mesh: dp: 16 (over z, y, core), mp: 2 (over x).
Axes of the slice: x: 2, y: 2, z: 4, core: 2. Of those that a mesh axis runs over, the one named last changes fastest.
Arguments:
- layer_input: bfloat16 [8192, 768], P('dp'), may hold values from -36 to 36
- memory: bfloat16 [8192, 768], P('dp'), may hold values from -6 to 6
- cotangent: bfloat16 [8192, 768], P('dp'), may hold values from -6 to 6
- dec_segments: int32 [16, 512], P('dp'), may hold values from 0 to 7, never falling along the last dimension, each value on 1 to 128 neighbouring positions
- mem_segments: int32 [16, 512], P('dp'), may hold values from 0 to 7, never falling along the last dimension, each value on 1 to 128 neighbouring positions
- w_query: bfloat16 [768, 768], P(None, 'mp'), may hold values from -0.0546875 to 0.0546875
- w_key: bfloat16 [768, 768], P(None, 'mp'), may hold values from -0.21875 to 0.21875
- w_value: bfloat16 [768, 768], P(None, 'mp'), may hold values from -0.21875 to 0.21875
- w_out: bfloat16 [768, 768], P('mp'), may hold values from -0.875 to 0.875
- c_query: bfloat16 [768, 768], P(None, 'mp'), may hold values from -0.0546875 to 0.0546875
- c_key: bfloat16 [768, 768], P(None, 'mp'), may hold values from -0.21875 to 0.21875
- c_value: bfloat16 [768, 768], P(None, 'mp'), may hold values from -0.21875 to 0.21875
- c_out: bfloat16 [768, 768], P('mp'), may hold values from -0.875 to 0.875
- w_gate: bfloat16 [768, 2048], P(None, 'mp'), may hold values from -0.21875 to 0.21875
- w_up: bfloat16 [768, 2048], P(None, 'mp'), may hold values from -0.21875 to 0.21875
- w_down: bfloat16 [2048, 768], P('mp'), may hold values from -0.1875 to 0.1875
- gain_self: bfloat16 [768], replicated, may hold values from 0.099609375 to 1.8984375
- gain_cross: bfloat16 [768], replicated, may hold values from 0.099609375 to 1.8984375
- gain_ffn: bfloat16 [768], replicated, may hold values from 0.099609375 to 1.8984375
- rel_bias: bfloat16 [32, 12], P(None, 'mp'), may hold values from -4 to 4
Outputs:
- output: bfloat16 [8192, 768], P('dp')
- input_grad: float32 [8192, 768], P('dp')
- memory_grad: float32 [8192, 768], P('dp', 'mp')
- w_query_grad: float32 [768, 768], P('dp', 'mp')
- w_key_grad: float32 [768, 768], P('dp', 'mp')
- w_value_grad: float32 [768, 768], P('dp', 'mp')
- w_out_grad: float32 [768, 768], P('mp', 'dp')
- c_query_grad: float32 [768, 768], P('dp', 'mp')
- c_key_grad: float32 [768, 768], P('dp', 'mp')
- c_value_grad: float32 [768, 768], P('dp', 'mp')
- c_out_grad: float32 [768, 768], P('mp', 'dp')
- w_gate_grad: float32 [768, 2048], P('dp', 'mp')
- w_up_grad: float32 [768, 2048], P('dp', 'mp')
- w_down_grad: float32 [2048, 768], P('mp', 'dp')
- gain_self_grad: float32 [768], P('dp')
- gain_cross_grad: float32 [768], P('dp')
- gain_ffn_grad: float32 [768], P('dp')
- rel_bias_grad: float32 [32, 12], P(None, 'mp')
The draws below stay inside these ranges and needn't reach their ends.
Inputs may be any that keep to these rules, and one draw needn't show every extreme that they name: `dec_segments`: in each row the documents are numbered 0 to 7 in order, each of 1 to 128 tokens, one of exactly 128; every number is present. `mem_segments`: in each row the documents are numbered 0 to 7 in order, each of 1 to 128 tokens, one of exactly 128; every number is present.
All inputs are finite; a program needn't handle non-finite values.
Results may differ from the reference program's by a relative error of at most 0.025.
The reference program's roundings to bfloat16 on the way count: a program that leaves them out, or rounds other values in their place, can miss the bound.
Values sent between devices are 32-bit elements; how exact they have to be, the bound alone decides.
No kernel may reach another device: no remote copies, remote signals or barrier semaphores. Data moves between devices by JAX's collectives and lax.ppermute only.
A program may use at most 192 MiB of HBM per device.

```python
import math
import jax
import jax.numpy as jnp
import numpy as np
from jax import lax

D = 768
H = 12
DK = 64
FF = 2048
NB = 32
MAXD = 128
L = 512
LM = 512
SEGS = 8
SEGMAX = 128
ROWS = 16
TOKENS = 8192
MTOK = 8192


def draw_layer_input(key, part):
    key = jax.random.fold_in(key, 11)
    normal_key, column_key, row_key = jax.random.split(key, 3)
    base = jnp.clip(jax.random.normal(normal_key, (TOKENS, D), jnp.float32), -6.0, 6.0)
    row_scale = jnp.exp(jax.random.uniform(row_key, (TOKENS, 1), jnp.float32, math.log(0.5), math.log(2.0)))
    column_scale = jnp.exp(jax.random.uniform(column_key, (1, D), jnp.float32, math.log(0.3), math.log(3.0)))
    return (base * column_scale * row_scale).astype(jnp.bfloat16)


def spiked(values, key, source, target, shards_of, factor):
    def block_of(dim):
        return (jnp.arange(values.shape[dim]) // (values.shape[dim] // shards_of)).reshape((-1,) + (1,) * (values.ndim - 1 - dim))

    first = jax.random.permutation(key, shards_of)[block_of(target)]
    far = (block_of(target) + shards_of // 2) % shards_of
    return jnp.where((block_of(source) == first) | (block_of(source) == far), factor * values, values)


def shard_levels(key, extent, cuts, low, high):
    def one(dim, parts):
        heights = jax.random.uniform(jax.random.fold_in(jax.random.fold_in(key, 6), dim), (parts,), jnp.float32, low / len(cuts), high / len(cuts))
        return jnp.repeat(jnp.exp(heights), extent[dim] // parts).reshape((-1,) + (1,) * (len(extent) - dim - 1))

    level = one(*cuts[0])
    for cut in cuts[1:]:
        level = level * one(*cut)
    return level


def profile(count, total, limit, slope):
    portions = [(1 << 20) // math.isqrt(standing ** slope) + 1 for standing in range(2, count + 1)]
    rest, holding = total - limit - (count - 1), [1] * (count - 1)
    while rest > 0:
        movable = [i for i in range(count - 1) if holding[i] < limit]
        whole, remaining = sum([portions[i] for i in movable]), rest
        for i in movable:
            more = min(limit - holding[i], max(1, remaining * portions[i] // whole), rest)
            holding[i] = holding[i] + more
            rest = rest - more
    return np.array([limit] + holding)


def ragged_sizes(stream_key, amount, total, reach, lean):
    if amount == 2:
        one = jax.random.randint(stream_key, (), max(1, total - reach), min(reach, total - 1) + 1)
        return jnp.stack([one, total - one])
    sizes = jnp.asarray(profile(amount, total, reach, lean), jnp.int32)
    pairs = (amount - 1) // 2
    donor, taker = sizes[1:1 + 2 * pairs:2], sizes[2:2 + 2 * pairs:2]
    slack = jnp.minimum(donor - 1, reach - taker)
    shifted = jax.random.randint(jax.random.fold_in(stream_key, 1), (pairs,), 0, 1 << 20) % (slack + 1)
    sizes = sizes.at[1:1 + 2 * pairs:2].set(donor - shifted).at[2:2 + 2 * pairs:2].set(taker + shifted)
    return sizes[jax.random.permutation(jax.random.fold_in(stream_key, 2), amount)]


def normal_values(stream_key, shape, deviation, most, cuts=(), dtype=jnp.bfloat16):
    entries = deviation * jax.random.normal(stream_key, shape, jnp.float32)
    if cuts:
        entries = entries * shard_levels(stream_key, shape, cuts, -0.22, 0.18)
    return jnp.clip(entries, -most, most).astype(dtype)


def bell_draw_with(own_key, dims, deviation, most, cuts, heavy, held_as=jnp.bfloat16):
    entries = deviation * jax.random.normal(own_key, dims, jnp.float32)
    if cuts:
        entries = entries * shard_levels(own_key, dims, cuts, -0.22, 0.18)
    return jnp.clip(spiked(entries, jax.random.fold_in(own_key, 3), *heavy), -most, most).astype(held_as)


def setup_inputs(seed: int = 0) -> dict:
    arg_keys = jax.random.split(jax.random.key(seed), 21)
    return {
        "layer_input": draw_layer_input(jax.random.fold_in(arg_keys[20], 71), 0),
        "memory": bell_draw_with(arg_keys[1], (MTOK, D), 1.0, 6.0, ((0, 16),), (0, 1, 16, 2.0)),
        "cotangent": bell_draw_with(arg_keys[2], (TOKENS, D), 1.0, 6.0, ((0, 16),), (0, 1, 16, 2.0)),
        "dec_segments": jax.vmap(lambda own: jnp.searchsorted(jnp.cumsum(ragged_sizes(own, SEGS, L, SEGMAX, 0)), jnp.arange(L), side="right"))(jax.random.split(arg_keys[3], ROWS)).reshape((ROWS, L)).astype(jnp.int32),
        "mem_segments": jax.vmap(lambda own: jnp.searchsorted(jnp.cumsum(ragged_sizes(own, SEGS, LM, SEGMAX, 0)), jnp.arange(LM), side="right"))(jax.random.split(arg_keys[4], ROWS)).reshape((ROWS, LM)).astype(jnp.int32),
        "w_query": normal_values(arg_keys[5], (D, H * DK), (D * 16) ** -0.5, 0.0546875, ((1, 2),)),
        "w_key": normal_values(arg_keys[6], (D, H * DK), D ** -0.5, 0.21875, ((1, 2),)),
        "w_value": normal_values(arg_keys[7], (D, H * DK), D ** -0.5, 0.21875, ((1, 2),)),
        "w_out": normal_values(arg_keys[8], (H * DK, D), (H * DK // 16) ** -0.5, 0.875, ((0, 2),)),
        "c_query": normal_values(arg_keys[9], (D, H * DK), (D * 16) ** -0.5, 0.0546875, ((1, 2),)),
        "c_key": normal_values(arg_keys[10], (D, H * DK), D ** -0.5, 0.21875, ((1, 2),)),
        "c_value": normal_values(arg_keys[11], (D, H * DK), D ** -0.5, 0.21875, ((1, 2),)),
        "c_out": normal_values(arg_keys[12], (H * DK, D), (H * DK // 16) ** -0.5, 0.875, ((0, 2),)),
        "w_gate": normal_values(arg_keys[13], (D, FF), D ** -0.5, 0.21875, ((1, 2),)),
        "w_up": normal_values(arg_keys[14], (D, FF), D ** -0.5, 0.21875, ((1, 2),)),
        "w_down": normal_values(arg_keys[15], (FF, D), (FF // 2) ** -0.5, 0.1875, ((0, 2),)),
        "gain_self": jnp.clip(1.0 + 0.18 * jax.random.normal(arg_keys[16], (D,), jnp.float32), 0.099609375, 1.8984375).astype(jnp.bfloat16),
        "gain_cross": jnp.clip(1.0 + 0.18 * jax.random.normal(arg_keys[17], (D,), jnp.float32), 0.099609375, 1.8984375).astype(jnp.bfloat16),
        "gain_ffn": jnp.clip(1.0 + 0.18 * jax.random.normal(arg_keys[18], (D,), jnp.float32), 0.099609375, 1.8984375).astype(jnp.bfloat16),
        "rel_bias": normal_values(arg_keys[19], (NB, H), 1.0, 4.0, ((1, 2),)),
    }


@jax.custom_vjp
def low(v):
    return lax.optimization_barrier(v.astype(jnp.bfloat16)).astype(jnp.float32)

@jax.custom_vjp
def low_back(v):
    return v

def low_keep(v):
    return (low(v), None)

def low_pass(kept, grad):
    return (grad,)

def back_keep(v):
    return (v, None)

def back_low(kept, grad):
    return (low(grad),)
low.defvjp(low_keep, low_pass)
low_back.defvjp(back_keep, back_low)
EPS = 1e-06
NEG = -1000000000.0
HIGHEST = lax.Precision.HIGHEST

def both_ways(v):
    return low_back(low(v))

def matmul(left, right):
    return jnp.dot(left, right, precision=HIGHEST)

def bucket_table(length):
    exact = NB // 2
    boundaries = [math.ceil(exact * (MAXD / exact) ** (step / exact)) for step in range(1, exact)]
    row_ids = lax.broadcasted_iota(jnp.int32, (length, length), 0)
    col_ids = lax.broadcasted_iota(jnp.int32, (length, length), 1)
    distance = jnp.maximum(row_ids - col_ids, 0)
    far_bucket = jnp.full((length, length), exact, jnp.int32)
    for boundary in boundaries:
        far_bucket = far_bucket + (distance >= boundary).astype(jnp.int32)
    return (jnp.where(distance < exact, distance, far_bucket), row_ids >= col_ids)

def rms_scale(stream, gain):
    return stream * lax.rsqrt(lax.optimization_barrier(jnp.mean(stream * stream, axis=-1, keepdims=True)) + EPS) * gain

def attend_row(queries, key_rows, value_rows, extra, allowed):
    scores = low_back(jnp.einsum('qhd,khd->hqk', queries, key_rows, precision=HIGHEST) + extra)
    scores = jnp.where(allowed[None], scores, NEG)
    largest = lax.optimization_barrier(jnp.max(scores, axis=-1, keepdims=True))
    expanded = jnp.exp(scores - largest)
    attention = low(expanded / lax.optimization_barrier(jnp.sum(expanded, axis=-1, keepdims=True)))
    return both_ways(jnp.einsum('hqk,khd->qhd', attention, value_rows, precision=HIGHEST))

def reference(layer_input, memory, cotangent, dec_segments, mem_segments, w_query, w_key, w_value, w_out, c_query, c_key, c_value, c_out, w_gate, w_up, w_down, gain_self, gain_cross, gain_ffn, rel_bias):
    rows_total = dec_segments.shape[0]
    group = math.gcd(rows_total, 8)
    group_count = rows_total // group
    params = tuple((weight.astype(jnp.float32) for weight in (w_query, w_key, w_value, w_out, c_query, c_key, c_value, c_out, w_gate, w_up, w_down, gain_self, gain_cross, gain_ffn, rel_bias)))
    bucket_ids, causal = bucket_table(L)

    def layer(stream, memory_rows, weights, dec_ids, mem_ids):
        query_w, key_w, value_w, out_w, cquery_w, ckey_w, cvalue_w, cout_w, gate_w, up_w, down_w, gain_one, gain_two, gain_three, bias_w = weights
        row_count = dec_ids.shape[0]
        token_count = stream.shape[0]
        normed_one = low(rms_scale(stream, gain_one))
        queries = both_ways(matmul(normed_one, query_w)).reshape(row_count, L, H, DK)
        key_rows = both_ways(matmul(normed_one, key_w)).reshape(row_count, L, H, DK)
        value_rows = both_ways(matmul(normed_one, value_w)).reshape(row_count, L, H, DK)
        bias_full = jnp.transpose(jnp.take(bias_w, bucket_ids, axis=0), (2, 0, 1))

        def self_row(items):
            allowed = causal & (items[3][:, None] == items[3][None, :])
            return attend_row(items[0], items[1], items[2], bias_full, allowed)
        self_mixed = lax.map(jax.checkpoint(self_row), (queries, key_rows, value_rows, dec_ids))
        stream_one = stream + low_back(matmul(self_mixed.reshape(token_count, H * DK), out_w))
        normed_two = low(rms_scale(stream_one, gain_two))
        cross_queries = both_ways(matmul(normed_two, cquery_w)).reshape(row_count, L, H, DK)
        cross_keys = both_ways(matmul(memory_rows, ckey_w)).reshape(row_count, LM, H, DK)
        cross_values = both_ways(matmul(memory_rows, cvalue_w)).reshape(row_count, LM, H, DK)

        def cross_row(items):
            allowed = items[3][:, None] == items[4][None, :]
            return attend_row(items[0], items[1], items[2], 0.0, allowed)
        cross_mixed = lax.map(jax.checkpoint(cross_row), (cross_queries, cross_keys, cross_values, dec_ids, mem_ids))
        stream_two = stream_one + low_back(matmul(cross_mixed.reshape(token_count, H * DK), cout_w))
        normed_three = low(rms_scale(stream_two, gain_three))
        gate_pre = low_back(matmul(normed_three, gate_w))
        up_pre = low_back(matmul(normed_three, up_w))
        hidden = low(jax.nn.gelu(gate_pre, approximate=True) * up_pre)
        return stream_two + low_back(matmul(hidden, down_w))

    def one_group(carry, items):
        stream, memory_rows, grad_out, dec_ids, mem_ids = items
        result, pullback = jax.vjp(lambda first, second, third: layer(first, second, third, dec_ids, mem_ids), stream, memory_rows, params)
        grad_stream, grad_memory, grad_params = pullback(grad_out)
        carry = jax.tree.map(lambda total, term: total + term, carry, grad_params)
        return (carry, (result.astype(jnp.bfloat16), grad_stream, grad_memory))
    zeros = jax.tree.map(jnp.zeros_like, params)
    inputs = (layer_input.astype(jnp.float32).reshape(group_count, group * L, D), memory.astype(jnp.float32).reshape(group_count, group * LM, D), cotangent.astype(jnp.float32).reshape(group_count, group * L, D), dec_segments.reshape(group_count, group, L), mem_segments.reshape(group_count, group, LM))
    totals, (outputs, input_grads, memory_grads) = lax.scan(one_group, zeros, inputs)
    return (outputs.reshape(TOKENS, D), input_grads.reshape(TOKENS, D), memory_grads.reshape(MTOK, D), totals[0], totals[1], totals[2], totals[3], totals[4], totals[5], totals[6], totals[7], totals[8], totals[9], totals[10], totals[11], totals[12], totals[13], totals[14])
```

```python
import math

import jax
import jax.numpy as jnp
from jax import lax
from jax.sharding import PartitionSpec as P

DK = 64
NB = 32
MAXD = 128


EPS = 1e-06
NEG = -1000000000.0


def bucket_table(length):
    exact = NB // 2
    boundaries = [math.ceil(exact * (MAXD / exact) ** (step / exact)) for step in range(1, exact)]
    row_ids = lax.broadcasted_iota(jnp.int32, (length, length), 0)
    col_ids = lax.broadcasted_iota(jnp.int32, (length, length), 1)
    distance = jnp.maximum(row_ids - col_ids, 0)
    far_bucket = jnp.full((length, length), exact, jnp.int32)
    for boundary in boundaries:
        far_bucket = far_bucket + (distance >= boundary).astype(jnp.int32)
    return (jnp.where(distance < exact, distance, far_bucket), row_ids >= col_ids)


def rms_scale(stream, gain):
    return stream * lax.rsqrt(jnp.mean(stream * stream, axis=-1, keepdims=True) + EPS) * gain


def gelu_tanh(values):
    return jax.nn.gelu(values, approximate=True)


def contract_rows(left, right):
    return lax.dot_general(
        left, right, (((0,), (0,)), ((), ())), preferred_element_type=jnp.float32
    )


def contract_cols(left, right):
    return lax.dot_general(
        left, right, (((1,), (1,)), ((), ())), preferred_element_type=jnp.float32
    )


def swap_over(values, axis, bit):
    size = lax.axis_size(axis)
    return lax.ppermute(values, axis, [(place, place ^ bit) for place in range(size)])


def branch_total(partial_sum):
    return partial_sum + swap_over(partial_sum, "mp", 1)


def back_total(partial_sum):
    return partial_sum + swap_over(partial_sum, "mp", 1)


def halving_order(size, turned):
    bits = []
    bit = 1
    while bit < size:
        bits.append(bit)
        bit *= 2
    if turned and len(bits) > 2:
        bits = bits[:1] + bits[2:] + bits[1:2]
    return bits


def scatter_total(values, turned=False):
    size = lax.axis_size("dp")
    place = lax.axis_index("dp")
    order = halving_order(size, turned)
    count = len(order)
    values = values.reshape((2,) * count + (values.shape[0] // size,) + values.shape[1:])
    left = sorted(order, reverse=True)
    for bit in order:
        axis = left.index(bit)
        mine = (place // bit) % 2
        kept = lax.dynamic_index_in_dim(values, mine, axis, keepdims=False)
        sent = lax.dynamic_index_in_dim(values, 1 - mine, axis, keepdims=False)
        values = kept + swap_over(sent, "dp", bit)
        left.remove(bit)
    return values


def whole_total(values):
    size = lax.axis_size("dp")
    for bit in halving_order(size, False):
        values = values + swap_over(values, "dp", bit)
    return values


def attend_row(queries, key_rows, value_rows, extra, allowed):
    scores = (
        jnp.einsum("qhd,khd->hqk", queries, key_rows, preferred_element_type=jnp.float32) + extra
    )
    scores = jnp.where(allowed[None], scores, NEG)
    largest = jnp.max(scores, axis=-1, keepdims=True)
    expanded = jnp.exp(scores - largest)
    denominator = jnp.sum(expanded, axis=-1, keepdims=True)
    attention = (expanded / denominator).astype(jnp.bfloat16)
    blended = jnp.einsum("hqk,khd->qhd", attention, value_rows, preferred_element_type=jnp.float32)
    return (blended.astype(jnp.bfloat16), largest[..., 0] + jnp.log(denominator[..., 0]))


def attend_back(queries, key_rows, value_rows, grad_blended, log_total, extra, allowed):
    scores = (
        jnp.einsum("qhd,khd->hqk", queries, key_rows, preferred_element_type=jnp.float32) + extra
    )
    scores = jnp.where(allowed[None], scores, NEG)
    attention = jnp.exp(scores - log_total[..., None])
    grad_values = jnp.einsum(
        "hqk,qhd->khd",
        attention.astype(jnp.bfloat16),
        grad_blended,
        preferred_element_type=jnp.float32,
    )
    grad_attention = jnp.einsum(
        "qhd,khd->hqk", grad_blended, value_rows, preferred_element_type=jnp.float32
    )
    inner_sum = jnp.sum(attention * grad_attention, axis=-1, keepdims=True)
    grad_scores = (attention * (grad_attention - inner_sum)).astype(jnp.bfloat16)
    grad_queries = jnp.einsum(
        "hqk,khd->qhd", grad_scores, key_rows, preferred_element_type=jnp.float32
    )
    grad_keys = jnp.einsum("hqk,qhd->khd", grad_scores, queries, preferred_element_type=jnp.float32)
    return (
        grad_queries.astype(jnp.bfloat16),
        grad_keys.astype(jnp.bfloat16),
        grad_values.astype(jnp.bfloat16),
        grad_scores,
    )


def on_device(
    layer_input,
    memory,
    cotangent,
    dec_segments,
    mem_segments,
    w_query,
    w_key,
    w_value,
    w_out,
    c_query,
    c_key,
    c_value,
    c_out,
    w_gate,
    w_up,
    w_down,
    gain_self,
    gain_cross,
    gain_ffn,
    rel_bias,
):
    row_count = dec_segments.shape[0]
    length = dec_segments.shape[1]
    mem_length = mem_segments.shape[1]
    head_count = rel_bias.shape[1]
    inner_width = w_query.shape[1]
    tokens = row_count * length
    mem_tokens = row_count * mem_length
    dec_shape = (row_count, length, head_count, DK)
    mem_shape = (row_count, mem_length, head_count, DK)
    bucket_ids, causal = bucket_table(length)
    one_hot = (
        bucket_ids.reshape(1, length * length) == lax.broadcasted_iota(jnp.int32, (NB, 1), 0)
    ).astype(jnp.bfloat16)
    bias_full = lax.dot_general(
        rel_bias, one_hot, (((0,), (0,)), ((), ())), preferred_element_type=jnp.float32
    ).reshape(head_count, length, length)
    gain_one = gain_self.astype(jnp.float32)
    gain_two = gain_cross.astype(jnp.float32)
    gain_three = gain_ffn.astype(jnp.float32)
    stream = layer_input.astype(jnp.float32)
    normed_one = rms_scale(stream, gain_one).astype(jnp.bfloat16)
    queries = (
        jnp.dot(normed_one, w_query, preferred_element_type=jnp.float32)
        .astype(jnp.bfloat16)
        .reshape(dec_shape)
    )
    key_rows = (
        jnp.dot(normed_one, w_key, preferred_element_type=jnp.float32)
        .astype(jnp.bfloat16)
        .reshape(dec_shape)
    )
    value_rows = (
        jnp.dot(normed_one, w_value, preferred_element_type=jnp.float32)
        .astype(jnp.bfloat16)
        .reshape(dec_shape)
    )

    def self_forward(items):
        allowed = causal & (items[3][:, None] == items[3][None, :])
        return attend_row(items[0], items[1], items[2], bias_full, allowed)

    self_mixed, self_logsum = lax.map(self_forward, (queries, key_rows, value_rows, dec_segments))
    self_flat = self_mixed.reshape(tokens, inner_width)
    stream_one = stream + branch_total(
        jnp.dot(self_flat, w_out, preferred_element_type=jnp.float32)
    )
    normed_two = rms_scale(stream_one, gain_two).astype(jnp.bfloat16)
    cross_queries = (
        jnp.dot(normed_two, c_query, preferred_element_type=jnp.float32)
        .astype(jnp.bfloat16)
        .reshape(dec_shape)
    )
    cross_keys = (
        jnp.dot(memory, c_key, preferred_element_type=jnp.float32)
        .astype(jnp.bfloat16)
        .reshape(mem_shape)
    )
    cross_values = (
        jnp.dot(memory, c_value, preferred_element_type=jnp.float32)
        .astype(jnp.bfloat16)
        .reshape(mem_shape)
    )

    def cross_forward(items):
        allowed = items[3][:, None] == items[4][None, :]
        return attend_row(items[0], items[1], items[2], 0.0, allowed)

    cross_mixed, cross_logsum = lax.map(
        cross_forward, (cross_queries, cross_keys, cross_values, dec_segments, mem_segments)
    )
    cross_flat = cross_mixed.reshape(tokens, inner_width)
    stream_two = stream_one + branch_total(
        jnp.dot(cross_flat, c_out, preferred_element_type=jnp.float32)
    )
    normed_three = rms_scale(stream_two, gain_three).astype(jnp.bfloat16)
    gate_pre = jnp.dot(normed_three, w_gate, preferred_element_type=jnp.float32)
    up_pre = jnp.dot(normed_three, w_up, preferred_element_type=jnp.float32)
    activated, gelu_back = jax.vjp(gelu_tanh, gate_pre)
    hidden = (activated * up_pre).astype(jnp.bfloat16)
    stream_three = stream_two + branch_total(
        jnp.dot(hidden, w_down, preferred_element_type=jnp.float32)
    )
    output = stream_three.astype(jnp.bfloat16)
    grad_three = cotangent.astype(jnp.float32)
    down_in = grad_three.astype(jnp.bfloat16)
    grad_down = contract_rows(down_in, hidden)
    grad_hidden = contract_cols(down_in, w_down)
    grad_gate = gelu_back(grad_hidden * up_pre)[0].astype(jnp.bfloat16)
    grad_up = (grad_hidden * activated).astype(jnp.bfloat16)
    grad_wgate = contract_rows(normed_three, grad_gate)
    grad_wup = contract_rows(normed_three, grad_up)
    ffn_normed_grad = back_total(contract_cols(grad_gate, w_gate) + contract_cols(grad_up, w_up))
    unused_three, norm_back_three = jax.vjp(rms_scale, stream_two, gain_three)
    stream_grad_three, grad_gain_three = norm_back_three(ffn_normed_grad)
    grad_two = grad_three + stream_grad_three
    cross_in = grad_two.astype(jnp.bfloat16)
    grad_cout = contract_rows(cross_in, cross_flat)
    cross_mixed_grad = contract_cols(cross_in, c_out).astype(jnp.bfloat16).reshape(dec_shape)

    def cross_backward(items):
        allowed = items[3][:, None] == items[4][None, :]
        result = attend_back(items[0], items[1], items[2], items[5], items[6], 0.0, allowed)
        return (result[0], result[1], result[2])

    grad_cq, grad_ck, grad_cv = lax.map(
        cross_backward,
        (
            cross_queries,
            cross_keys,
            cross_values,
            dec_segments,
            mem_segments,
            cross_mixed_grad,
            cross_logsum,
        ),
    )
    grad_cq = grad_cq.reshape(tokens, inner_width)
    grad_ck = grad_ck.reshape(mem_tokens, inner_width)
    grad_cv = grad_cv.reshape(mem_tokens, inner_width)
    grad_cquery = contract_rows(normed_two, grad_cq)
    grad_ckey = contract_rows(memory, grad_ck)
    grad_cvalue = contract_rows(memory, grad_cv)
    memory_partial = contract_cols(grad_ck, c_key) + contract_cols(grad_cv, c_value)
    half = memory_partial.shape[1] // 2
    side = lax.axis_index("mp")
    memory_grad = lax.dynamic_slice_in_dim(memory_partial, side * half, half, 1) + swap_over(
        lax.dynamic_slice_in_dim(memory_partial, (1 - side) * half, half, 1), "mp", 1
    )
    cross_normed_grad = back_total(contract_cols(grad_cq, c_query))
    unused_two, norm_back_two = jax.vjp(rms_scale, stream_one, gain_two)
    stream_grad_two, grad_gain_two = norm_back_two(cross_normed_grad)
    grad_one = grad_two + stream_grad_two
    self_in = grad_one.astype(jnp.bfloat16)
    grad_wout = contract_rows(self_in, self_flat)
    self_mixed_grad = contract_cols(self_in, w_out).astype(jnp.bfloat16).reshape(dec_shape)

    def self_backward(items):
        allowed = causal & (items[3][:, None] == items[3][None, :])
        result = attend_back(items[0], items[1], items[2], items[4], items[5], bias_full, allowed)
        bias_piece = contract_cols(result[3].reshape(head_count, length * length), one_hot)
        return (result[0], result[1], result[2], bias_piece)

    grad_sq, grad_sk, grad_sv, bias_pieces = lax.map(
        self_backward, (queries, key_rows, value_rows, dec_segments, self_mixed_grad, self_logsum)
    )
    grad_sq = grad_sq.reshape(tokens, inner_width)
    grad_sk = grad_sk.reshape(tokens, inner_width)
    grad_sv = grad_sv.reshape(tokens, inner_width)
    grad_wquery = contract_rows(normed_one, grad_sq)
    grad_wkey = contract_rows(normed_one, grad_sk)
    grad_wvalue = contract_rows(normed_one, grad_sv)
    self_normed_grad = back_total(
        contract_cols(grad_sq, w_query)
        + contract_cols(grad_sk, w_key)
        + contract_cols(grad_sv, w_value)
    )
    unused_one, norm_back_one = jax.vjp(rms_scale, stream, gain_one)
    stream_grad_one, grad_gain_one = norm_back_one(self_normed_grad)
    input_grad = grad_one + stream_grad_one
    bias_grad = whole_total(jnp.sum(bias_pieces, axis=0).T)
    shared_down = scatter_total(grad_down).T
    shared_gate = scatter_total(grad_wgate, True)
    shared_up = scatter_total(grad_wup)
    shared_cout = scatter_total(grad_cout).T
    shared_cquery = scatter_total(grad_cquery)
    shared_ckey = scatter_total(grad_ckey)
    shared_cvalue = scatter_total(grad_cvalue, True)
    shared_out = scatter_total(grad_wout).T
    shared_query = scatter_total(grad_wquery)
    shared_key = scatter_total(grad_wkey)
    shared_value = scatter_total(grad_wvalue, True)
    gains = scatter_total(
        jnp.stack((grad_gain_one, grad_gain_two, grad_gain_three), axis=1)
    )
    shared_gain_one = gains[:, 0]
    shared_gain_two = gains[:, 1]
    shared_gain_three = gains[:, 2]
    return (
        output,
        input_grad,
        memory_grad,
        shared_query,
        shared_key,
        shared_value,
        shared_out,
        shared_cquery,
        shared_ckey,
        shared_cvalue,
        shared_cout,
        shared_gate,
        shared_up,
        shared_down,
        shared_gain_one,
        shared_gain_two,
        shared_gain_three,
        bias_grad,
    )


def solution(mesh):
    return jax.shard_map(
        on_device,
        mesh=mesh,
        in_specs=(
            P("dp", None),
            P("dp", None),
            P("dp", None),
            P("dp", None),
            P("dp", None),
            P(None, "mp"),
            P(None, "mp"),
            P(None, "mp"),
            P("mp", None),
            P(None, "mp"),
            P(None, "mp"),
            P(None, "mp"),
            P("mp", None),
            P(None, "mp"),
            P(None, "mp"),
            P("mp", None),
            P(),
            P(),
            P(),
            P(None, "mp"),
        ),
        out_specs=(
            P("dp", None),
            P("dp", None),
            P("dp", "mp"),
            P("dp", "mp"),
            P("dp", "mp"),
            P("dp", "mp"),
            P("mp", "dp"),
            P("dp", "mp"),
            P("dp", "mp"),
            P("dp", "mp"),
            P("mp", "dp"),
            P("dp", "mp"),
            P("dp", "mp"),
            P("mp", "dp"),
            P("dp"),
            P("dp"),
            P("dp"),
            P(None, "mp"),
        ),
        check_vma=False,
    )
```
